32 devices in a mesh: contour: 4 (over y, x), clus: 8 (over z, core).
Axes of the slice: x: 2, y: 2, z: 4, core: 2. Of those that a mesh axis runs over, the one named last changes fastest.
Arguments:
- probes: float32 [64, 2, 16, 128], P('clus'), may hold values from -18 to 18
- near_blocks: bfloat16 [256, 27, 2, 128, 128], P(('contour', 'clus')), parts along dimension 0
- near_list: int32 [64, 27], P('clus'), may hold values from 0 to 63, as said below
- near_count: int32 [64], P('clus'), may hold values from 1 to 27
- cluster_rows: int32 [64], P('clus'), may hold values from 64 to 128
- row_basis: bfloat16 [256, 2, 32, 128], P(('contour', 'clus')), parts along dimension 0, may hold values from -1 to 1
- col_basis: bfloat16 [256, 2, 32, 128], P(('contour', 'clus')), parts along dimension 0, may hold values from -0.5 to 0.5
- far_list: int32 [64, 32], P('clus'), may hold values from 0 to 63, as said below
- far_coupling: float32 [256, 32, 2, 32, 32], P(('contour', 'clus')), parts along dimension 0, may hold values from -0.375 to 0.375
- weight: float32 [8], P('contour'), parts along dimension 0, may hold values from -6 to 6
Outputs:
- solution: float32 [256, 2, 16, 128], P(('contour', 'clus')), parts along dimension 0
- moment: float32 [8, 16, 16], P('contour'), parts along dimension 0
- arnoldi: float32 [16, 16], P('contour'), parts along dimension 0
The draws below stay inside these ranges and needn't reach their ends.
There are 4 independent parts, one for each index of `contour`. The reference program is written for one: setup_inputs(seed, part) draws one part's arguments, and reference() takes and returns one part's arrays. A program takes and returns all parts, laid end to end along the dimension named above; an argument that names none is the same for every part. Nothing has to cross between parts.
Inputs may be any that keep to these rules, and one draw needn't show every extreme that they name: near_list[i, 0] = i; every entry lies within 8 clusters of i. `far_list`: every entry j of cluster i's list has min(|j - i|, 64 - |j - i|) > 8, so no far slot names a cluster of i's near list.
All inputs are finite; a program needn't handle non-finite values.
Results may differ from the reference program's by a relative error of at most 0.0019.
Values may be sent and summed in bfloat16 or wider, within the bound.
A program may use at most 128 MiB of HBM per device.

```python
import jax
import jax.numpy as jnp
from jax import lax

BS = 128
RANK = 32
PROBES = 16
KMAX = 27
FMAX = 32
NB_DEV = 8
CLUSTERS = 64


def draw_probes(key, part):
    shape = (CLUSTERS, 2, PROBES, BS)
    place = lax.broadcasted_iota(jnp.int32, shape, 0).astype(jnp.float32) / (CLUSTERS - 1)
    noise = jnp.clip(jax.random.normal(key, shape, jnp.float32), -6.0, 6.0)
    values = noise * (1.0 + 2.0 * place)
    return values.astype(jnp.float32)


def draw_near_blocks(key, part):
    key_one, key_two, key_three = jax.random.split(key, 3)
    shape = (CLUSTERS, KMAX, 2, BS, BS)
    spread = 0.5 / (BS * KMAX) ** 0.5
    noise = jax.random.normal(key_one, shape, jnp.float32) * spread
    diag_re = jax.random.uniform(key_two, (CLUSTERS, BS), jnp.float32, 2.5, 3.5)
    diag_im = jax.random.uniform(key_three, (CLUSTERS, BS), jnp.float32, -1.0, 1.0)
    eye = (lax.broadcasted_iota(jnp.int32, (BS, BS), 0) == lax.broadcasted_iota(jnp.int32, (BS, BS), 1)).astype(jnp.float32)
    noise = noise.at[:, 0, 0].add(diag_re[:, :, None] * eye[None])
    noise = noise.at[:, 0, 1].add(diag_im[:, :, None] * eye[None])
    return noise.astype(jnp.bfloat16)


def draw_near_list(key, part):
    offsets = jax.random.randint(key, (CLUSTERS, KMAX), -NB_DEV, NB_DEV + 1)
    offsets = offsets.at[:, 0].set(0)
    base = lax.broadcasted_iota(jnp.int32, (CLUSTERS, KMAX), 0)
    return jnp.clip(base + offsets, 0, CLUSTERS - 1).astype(jnp.int32)


def draw_near_count(key, part):
    counts = jax.random.randint(key, (CLUSTERS,), 1, KMAX + 1)
    owner = lax.broadcasted_iota(jnp.int32, (CLUSTERS,), 0) // NB_DEV
    boost = jnp.where(owner % 4 == 0, KMAX // 2, 0)
    counts = jnp.clip(counts + boost, 1, KMAX)
    return counts.at[0].set(KMAX).at[1].set(1).astype(jnp.int32)


def draw_cluster_rows(key, part):
    rows = jax.random.randint(key, (CLUSTERS,), BS // 2, BS + 1)
    return rows.at[0].set(BS).at[1].set(BS // 2).astype(jnp.int32)


def draw_far_list(key, part):
    offsets = jax.random.randint(key, (CLUSTERS, FMAX), NB_DEV + 1, CLUSTERS - NB_DEV)
    base = lax.broadcasted_iota(jnp.int32, (CLUSTERS, FMAX), 0)
    return ((base + offsets) % CLUSTERS).astype(jnp.int32)


def steps_of(rng, dims, cuts, smallest, top_value):
    loudness = 1.0
    for position, parts in cuts:
        steps = jax.random.uniform(jax.random.fold_in(jax.random.fold_in(rng, 6), position), (parts,), jnp.float32, smallest / len(cuts), top_value / len(cuts))
        loudness = loudness * jnp.repeat(jnp.exp(steps), dims[position] // parts).reshape((-1,) + (1,) * (len(dims) - 1 - position))
    return loudness


def gaussian(key, dims, width, reach, cuts=(), held_as=jnp.bfloat16):
    drawn = width * jax.random.normal(key, dims, jnp.float32)
    if cuts:
        drawn = drawn * steps_of(key, dims, cuts, -0.22, 0.18)
    return jnp.clip(drawn, -reach, reach).astype(held_as)


def setup_inputs(seed: int = 0, part: int = 0) -> dict:
    key_list = jax.random.split(jax.random.key(seed), 11)
    part_keys = jax.random.split(jax.random.fold_in(key_list[10], part), 11)
    probes = draw_probes(jax.random.fold_in(key_list[10], 71), part)
    near_blocks = draw_near_blocks(jax.random.fold_in(jax.random.fold_in(key_list[10], part), 71), part)
    near_list = draw_near_list(jax.random.fold_in(key_list[10], 71), part)
    near_count = draw_near_count(jax.random.fold_in(key_list[10], 71), part)
    cluster_rows = draw_cluster_rows(jax.random.fold_in(key_list[10], 71), part)
    row_basis = gaussian(part_keys[5], (CLUSTERS, 2, RANK, BS), RANK ** -0.5, 1.0, ((0, 8),))
    col_basis = gaussian(part_keys[6], (CLUSTERS, 2, RANK, BS), BS ** -0.5, 0.5, ((0, 8),))
    far_list = draw_far_list(jax.random.fold_in(key_list[10], 71), part)
    far_coupling = gaussian(part_keys[8], (CLUSTERS, FMAX, 2, RANK, RANK), (RANK * FMAX // 4) ** -0.5, 0.375, ((0, 8),), jnp.float32)
    weight = gaussian(part_keys[9], (2,), 2.0, 6.0, (), jnp.float32)
    return dict(probes=probes, near_blocks=near_blocks, near_list=near_list, near_count=near_count, cluster_rows=cluster_rows, row_basis=row_basis, col_basis=col_basis, far_list=far_list, far_coupling=far_coupling, weight=weight)


def operate(field, row_mask, near_blocks, near_list, slot_live, row_basis, col_basis, far_list, far_coupling):
    narrow = field.astype(jnp.bfloat16)
    pulled = narrow[near_list]
    pulled = jnp.where(slot_live[:, :, None, None, None], pulled, jnp.zeros((), jnp.bfloat16)).astype(jnp.float32)
    blocks = near_blocks.astype(jnp.float32)

    def prod(mat, vec):
        return jnp.einsum('nkrs,nkps->npr', mat, vec)
    near_re = prod(blocks[:, :, 0], pulled[:, :, 0]) - prod(blocks[:, :, 1], pulled[:, :, 1])
    near_im = prod(blocks[:, :, 0], pulled[:, :, 1]) + prod(blocks[:, :, 1], pulled[:, :, 0])
    basis = col_basis.astype(jnp.float32)
    wide = narrow.astype(jnp.float32)

    def contract(mat, vec):
        return jnp.einsum('nqr,npr->nqp', mat, vec)
    coef_re = contract(basis[:, 0], wide[:, 0]) - contract(basis[:, 1], wide[:, 1])
    coef_im = contract(basis[:, 0], wide[:, 1]) + contract(basis[:, 1], wide[:, 0])
    taken_re = coef_re[far_list]
    taken_im = coef_im[far_list]

    def couple(mat, vec):
        return jnp.einsum('nfqs,nfsp->nqp', mat, vec, precision=lax.Precision.HIGHEST)
    far_re = couple(far_coupling[:, :, 0], taken_re) - couple(far_coupling[:, :, 1], taken_im)
    far_im = couple(far_coupling[:, :, 0], taken_im) + couple(far_coupling[:, :, 1], taken_re)
    far_re = far_re.astype(jnp.bfloat16).astype(jnp.float32)
    far_im = far_im.astype(jnp.bfloat16).astype(jnp.float32)
    rows = row_basis.astype(jnp.float32)

    def expand(mat, vec):
        return jnp.einsum('nqr,nqp->npr', mat, vec)
    out_re = expand(rows[:, 0], far_re) - expand(rows[:, 1], far_im)
    out_im = expand(rows[:, 0], far_im) + expand(rows[:, 1], far_re)
    total = jnp.stack([near_re + out_re, near_im + out_im], axis=1)
    return total * row_mask

def inner(left, right):
    real_part = lax.optimization_barrier(jnp.sum(left[:, 0] * right[:, 0] + left[:, 1] * right[:, 1], axis=(0, 2)))
    imag_part = lax.optimization_barrier(jnp.sum(left[:, 0] * right[:, 1] - left[:, 1] * right[:, 0], axis=(0, 2)))
    return (real_part, imag_part)

def scaled(field, real_part, imag_part):
    sr = real_part[None, :, None]
    si = imag_part[None, :, None]
    return jnp.stack([sr * field[:, 0] - si * field[:, 1], sr * field[:, 1] + si * field[:, 0]], axis=1)

def reference(probes, near_blocks, near_list, near_count, cluster_rows, row_basis, col_basis, far_list, far_coupling, weight):
    rows_iota = lax.broadcasted_iota(jnp.int32, (probes.shape[0], probes.shape[3]), 1)
    row_mask = (rows_iota < cluster_rows[:, None]).astype(jnp.float32)[:, None, None, :]
    slots_iota = lax.broadcasted_iota(jnp.int32, near_list.shape, 1)
    slot_live = slots_iota < near_count[:, None]
    base = probes * row_mask

    def apply(field):
        return operate(field, row_mask, near_blocks, near_list, slot_live, row_basis, col_basis, far_list, far_coupling)
    beta = jnp.sqrt(lax.optimization_barrier(jnp.sum(base * base, axis=(0, 1, 3))) + 1e-06)
    first = base / beta[None, None, :, None]
    image_one = apply(first)
    proj_re, proj_im = inner(first, image_one)
    remain = image_one - scaled(first, proj_re, proj_im)
    size_two = jnp.sqrt(lax.optimization_barrier(jnp.sum(remain * remain, axis=(0, 1, 3))) + 1e-06)
    second = remain / size_two[None, None, :, None]
    factor = 1.0 / (CLUSTERS * BS)
    arnoldi = jnp.stack([beta * jnp.sqrt(jnp.float32(factor)), proj_re, proj_im, size_two], axis=0)
    image_two = apply(second)
    g11, zero_one = inner(image_one, image_one)
    g22, zero_two = inner(image_two, image_two)
    g12r, g12i = inner(image_one, image_two)
    q1r, q1i = inner(image_one, base)
    q2r, q2i = inner(image_two, base)
    det = g11 * g22 - (g12r * g12r + g12i * g12i)
    y1r = (g22 * q1r - (g12r * q2r - g12i * q2i)) / det
    y1i = (g22 * q1i - (g12r * q2i + g12i * q2r)) / det
    y2r = (g11 * q2r - (g12r * q1r + g12i * q1i)) / det
    y2i = (g11 * q2i - (g12r * q1i - g12i * q1r)) / det
    iterate = scaled(first, y1r, y1i) + scaled(second, y2r, y2i)
    wr = weight[0]
    wi = weight[1]
    solution = jnp.stack([wr * iterate[:, 0] - wi * iterate[:, 1], wr * iterate[:, 1] + wi * iterate[:, 0]], axis=1)
    mom_re = jnp.einsum('npr,nqr->pq', base[:, 0], iterate[:, 0], precision=lax.Precision.HIGHEST) + jnp.einsum('npr,nqr->pq', base[:, 1], iterate[:, 1], precision=lax.Precision.HIGHEST)
    mom_im = jnp.einsum('npr,nqr->pq', base[:, 0], iterate[:, 1], precision=lax.Precision.HIGHEST) - jnp.einsum('npr,nqr->pq', base[:, 1], iterate[:, 0], precision=lax.Precision.HIGHEST)
    moment = jnp.stack([wr * mom_re - wi * mom_im, wr * mom_im + wi * mom_re], axis=0) * factor
    return (solution, moment, arnoldi)
```

```python
import functools

import jax
import jax.numpy as jnp
from jax import lax
from jax.experimental import pallas as pl
from jax.experimental.pallas import tpu as pltpu
from jax.sharding import PartitionSpec as P

MESH = pl.DeviceIdType.MESH
F32 = jnp.float32
BF16 = jnp.bfloat16
BETA, PROJ, NORM, GRAM, COEF, HALO = 0, 1, 2, 3, 4, 6


def dot_nt(left, right, precision=None):
    return lax.dot_general(
        left, right, (((1,), (1,)), ((), ())), precision=precision, preferred_element_type=F32
    )


def joined(prod, half, lanes):
    re = prod[:half, :lanes] - prod[half:, lanes:]
    im = prod[half:, :lanes] + prod[:half, lanes:]
    return jnp.concatenate([re, im], axis=0)


def kernel(
    n,
    near_list,
    near_count,
    cluster_rows,
    far_list,
    weight,
    probes,
    row_basis,
    col_basis,
    near_hbm,
    far_hbm,
    solution_ref,
    moment_ref,
    arnoldi_ref,
    near_v,
    far_v,
    wide_hi,
    wide_lo,
    col_pad,
    xs,
    raw,
    spread,
    total,
    base,
    first,
    second,
    image_one,
    image_two,
    beta_s,
    proj_s,
    norm_s,
    gram_s,
    near_sem,
    far_sem,
    send_sem,
    recv_sem,
):
    owned, rows, width = probes.shape
    half = rows // 2
    slots = near_v.shape[1]
    fslots = far_v.shape[1]
    rank = far_v.shape[3]
    per = width // rank
    me = lax.axis_index("clus")

    def near_copy(i):
        return pltpu.make_async_copy(near_hbm.at[i], near_v.at[i], near_sem.at[i])

    def far_copy(i):
        return pltpu.make_async_copy(far_hbm.at[i], far_v.at[i], far_sem.at[i])

    for i in range(owned):
        far_copy(i).start()
    for i in range(owned):
        near_copy(i).start()

    barrier = pltpu.get_barrier_semaphore()
    for o in range(1, n):
        pl.semaphore_signal(
            barrier, inc=1, device_id={"clus": lax.rem(me + o, n)}, device_id_type=MESH
        )
    pl.semaphore_wait(barrier, n - 1)

    def share(buf, phase):
        def copy(slot, o):
            return pltpu.make_async_remote_copy(
                src_ref=buf.at[slot],
                dst_ref=buf.at[slot],
                send_sem=send_sem.at[phase, o],
                recv_sem=recv_sem.at[phase, o],
                device_id={"clus": lax.rem(me + o, n)},
                device_id_type=MESH,
            )

        for o in range(1, n):
            copy(me, o).start()

        def finish():
            for o in range(1, n):
                copy(lax.rem(me + n - o, n), o).wait_recv()
            for o in range(1, n):
                copy(me, o).wait_send()

        return finish

    def summed(buf):
        out = buf[0]
        for d in range(1, n):
            out = out + buf[d]
        return out

    def lane_sum(v):
        return jnp.sum(v, axis=1, keepdims=True)

    def square_part(ref):
        acc = jnp.zeros((rows, width), F32)
        for i in range(owned):
            v = ref[i]
            acc = acc + v * v
        return acc[:half] + acc[half:]

    def inner_part(left, right):
        re = jnp.zeros((half, width), F32)
        im = jnp.zeros((half, width), F32)
        for i in range(owned):
            lr, li = left[i, :half], left[i, half:]
            rr, ri = right[i, :half], right[i, half:]
            re = re + (lr * rr + li * ri)
            im = im + (lr * ri - li * rr)
        return re, im

    lane = lax.broadcasted_iota(jnp.int32, (rows, width), 1)
    for i in range(owned):
        base[i] = jnp.where(lane < cluster_rows[i], probes[i], 0.0)
    beta_s[me] = square_part(base)
    finish_beta = share(beta_s, BETA)

    col_pad[...] = jnp.zeros_like(col_pad)
    for i in range(owned):
        at = (i % per) * rank
        col_pad[i, at : at + rank] = col_basis[i, 0]
        col_pad[i, width + at : width + at + rank] = col_basis[i, 1]
    for op in range(2):
        xs[op, 3 * owned] = jnp.zeros((rows, width), BF16)

    def lay(i, carry):
        far_copy(i).wait()
        for g in range(fslots // per):
            for c in range(2):
                tile = jnp.concatenate([far_v[i, g * per + a, c] for a in range(per)], axis=1)
                hi = tile.astype(BF16)
                wide_hi[i, c, g] = hi
                wide_lo[i, c, g] = (tile - hi.astype(F32)).astype(BF16)
        return carry

    lax.fori_loop(0, owned, lay, 0)

    finish_beta()
    beta = jnp.sqrt(lane_sum(summed(beta_s)) + 1e-06)
    beta_rows = jnp.concatenate([beta, beta], axis=0)

    def operate(op, field, image, meanwhile):
        def halo(o, src, dst, to):
            return pltpu.make_async_remote_copy(
                src_ref=xs.at[op, pl.ds(src * owned, owned)],
                dst_ref=xs.at[op, pl.ds(dst * owned, owned)],
                send_sem=send_sem.at[HALO + op, o],
                recv_sem=recv_sem.at[HALO + op, o],
                device_id={"clus": to},
                device_id_type=MESH,
            )

        right, left = lax.rem(me + 1, n), lax.rem(me + n - 1, n)
        for i in range(owned):
            xs[op, owned + i] = field[i].astype(BF16)
        halo(0, 1, 0, right).start()
        halo(1, 1, 2, left).start()
        for g in range(owned // per):
            prod = jnp.zeros((rows, 2 * width), F32)
            for a in range(per):
                prod = prod + dot_nt(xs[op, owned + g * per + a], col_pad[g * per + a])
            raw[op, me, g] = joined(prod, half, width)
        finish_coef = share(raw.at[op], COEF + op)
        meanwhile()
        halo(0, 1, 0, right).wait_recv()
        halo(1, 1, 2, left).wait_recv()
        shift = (me - 1) * owned

        def near(i, carry):
            if op == 0:
                near_copy(i).wait()
            count = near_count[i]

            def pulled(k):
                at = jnp.where(k < count, near_list[i, k] - shift, 3 * owned)
                return xs[op, at]

            acc = jnp.zeros((rows, 2 * width), F32)
            for k in range(0, slots - 1, 2):
                lhs = jnp.concatenate([pulled(k), pulled(k + 1)], axis=1)
                rhs = jnp.concatenate([near_v[i, k], near_v[i, k + 1]], axis=1)
                acc = acc + dot_nt(lhs, rhs)
            if slots % 2:
                acc = acc + dot_nt(pulled(slots - 1), near_v[i, slots - 1])
            total[i] = acc
            return carry

        lax.fori_loop(0, owned, near, 0)
        finish_coef()

        def expand(d, carry):
            for g in range(owned // per):
                tile = raw[op, d, g]
                for a in range(per):
                    m = jnp.where((lane >= a * rank) & (lane < (a + 1) * rank), tile, 0.0)
                    step = width // 2
                    while step >= rank:
                        m = m + pltpu.roll(m, step, 1)
                        step //= 2
                    spread[d * owned + g * per + a] = m
            return carry

        lax.fori_loop(0, n, expand, 0)

        def far(i, carry):
            acc_r = jnp.zeros((rows, rank), F32)
            acc_i = jnp.zeros((rows, rank), F32)
            for g in range(fslots // per):
                t = spread[far_list[i, g * per]]
                for a in range(1, per):
                    t = jnp.where(lane >= a * rank, spread[far_list[i, g * per + a]], t)
                hi = t.astype(BF16)
                lo = (t - hi.astype(F32)).astype(BF16)
                wr, wi = wide_hi[i, 0, g], wide_hi[i, 1, g]
                acc_r = acc_r + (dot_nt(hi, wr) + (dot_nt(lo, wr) + dot_nt(hi, wide_lo[i, 0, g])))
                acc_i = acc_i + (dot_nt(hi, wi) + (dot_nt(lo, wi) + dot_nt(hi, wide_lo[i, 1, g])))
            fr = acc_r[:half] - acc_i[half:]
            fi = acc_r[half:] + acc_i[:half]
            coef = jnp.concatenate([fr, fi], axis=0).astype(BF16)
            basis = jnp.concatenate([row_basis[i, 0], row_basis[i, 1]], axis=1)
            prod = total[i] + jnp.dot(coef, basis, preferred_element_type=F32)
            image[i] = jnp.where(lane < cluster_rows[i], joined(prod, half, width), 0.0)
            return carry

        lax.fori_loop(0, owned, far, 0)
        halo(0, 1, 0, right).wait_send()
        halo(1, 1, 2, left).wait_send()

    for i in range(owned):
        first[i] = base[i] / beta_rows
    operate(0, first, image_one, lambda: None)

    re, im = inner_part(first, image_one)
    proj_s[me, :half] = re
    proj_s[me, half:] = im
    share(proj_s, PROJ)()
    proj = lane_sum(summed(proj_s))
    pr, pi = proj[:half], proj[half:]
    for i in range(owned):
        fr, fi = first[i, :half], first[i, half:]
        second[i, :half] = image_one[i, :half] - (pr * fr - pi * fi)
        second[i, half:] = image_one[i, half:] - (pr * fi + pi * fr)
    norm_s[me] = square_part(second)
    share(norm_s, NORM)()
    size_two = jnp.sqrt(lane_sum(summed(norm_s)) + 1e-06)
    size_rows = jnp.concatenate([size_two, size_two], axis=0)
    for i in range(owned):
        second[i] = second[i] / size_rows

    def moments():
        m1 = jnp.zeros((rows, rows), F32)
        m2 = jnp.zeros((rows, rows), F32)
        for i in range(owned):
            m1 = m1 + dot_nt(base[i], first[i], lax.Precision.HIGHEST)
            m2 = m2 + dot_nt(base[i], second[i], lax.Precision.HIGHEST)
        gram_s[me] = jnp.zeros(gram_s.shape[1:], F32)
        gram_s[me, half : half + rows, :rows] = m1
        gram_s[me, half + rows :, :rows] = m2

    operate(1, second, image_two, moments)

    parts = (
        square_part(image_one),
        square_part(image_two),
        *inner_part(image_one, image_two),
        *inner_part(image_one, base),
        *inner_part(image_two, base),
    )
    narrow = lax.broadcasted_iota(jnp.int32, (half, width), 1)
    packed = jnp.zeros((half, width), F32)
    for k, part in enumerate(parts):
        packed = jnp.where(narrow == k, lane_sum(part), packed)
    gram_s[me, :half] = packed
    share(gram_s, GRAM)()
    gram = summed(gram_s)
    g11, g22, g12r, g12i, q1r, q1i, q2r, q2i = (
        lane_sum(jnp.where(narrow == k, gram[:half], 0.0)) for k in range(8)
    )
    det = g11 * g22 - (g12r * g12r + g12i * g12i)
    y1r = (g22 * q1r - (g12r * q2r - g12i * q2i)) / det
    y1i = (g22 * q1i - (g12r * q2i + g12i * q2r)) / det
    y2r = (g11 * q2r - (g12r * q1r + g12i * q1i)) / det
    y2i = (g11 * q2i - (g12r * q1i - g12i * q1r)) / det
    wr, wi = weight[0], weight[1]
    y1r, y1i = wr * y1r - wi * y1i, wr * y1i + wi * y1r
    y2r, y2i = wr * y2r - wi * y2i, wr * y2i + wi * y2r
    for i in range(owned):
        fr, fi = first[i, :half], first[i, half:]
        sr, si = second[i, :half], second[i, half:]
        solution_ref[i, :half] = (y1r * fr - y1i * fi) + (y2r * sr - y2i * si)
        solution_ref[i, half:] = (y1r * fi + y1i * fr) + (y2r * si + y2i * sr)

    eye = lax.broadcasted_iota(jnp.int32, (half, half), 0) == lax.broadcasted_iota(
        jnp.int32, (half, half), 1
    )

    def as_row(column):
        return jnp.sum(jnp.where(eye, column, 0.0), axis=0, keepdims=True)

    factor = 1.0 / (n * owned * width)
    arnoldi_ref[0:1] = as_row(beta * jnp.sqrt(F32(factor)))
    arnoldi_ref[1:2] = as_row(pr)
    arnoldi_ref[2:3] = as_row(pi)
    arnoldi_ref[3:4] = as_row(size_two)

    def moment_of(m):
        re = m[:half, :half] + m[half:, half:rows]
        im = m[:half, half:rows] - m[half:, :half]
        return re, im

    m1r, m1i = moment_of(gram[half : half + rows])
    m2r, m2i = moment_of(gram[half + rows :])
    y1r, y1i, y2r, y2i = as_row(y1r), as_row(y1i), as_row(y2r), as_row(y2i)
    moment_ref[0] = ((y1r * m1r - y1i * m1i) + (y2r * m2r - y2i * m2i)) * factor
    moment_ref[1] = ((y1r * m1i + y1i * m1r) + (y2r * m2i + y2i * m2r)) * factor


def shards(
    n,
    probes,
    near_blocks,
    near_list,
    near_count,
    cluster_rows,
    row_basis,
    col_basis,
    far_list,
    far_coupling,
    weight,
):
    owned, _, nprobe, width = probes.shape
    rows = 2 * nprobe
    slots = near_blocks.shape[1]
    fslots = far_coupling.shape[1]
    rank = far_coupling.shape[3]
    per = width // rank
    groups = fslots // per
    smem = pl.BlockSpec(memory_space=pltpu.SMEM)
    vmem = pl.BlockSpec(memory_space=pltpu.VMEM)
    hbm = pl.BlockSpec(memory_space=pl.ANY)
    field = pltpu.VMEM((owned, rows, width), F32)
    sol, moment, arnoldi = pl.pallas_call(
        functools.partial(kernel, n),
        out_shape=(
            jax.ShapeDtypeStruct((owned, rows, width), F32),
            jax.ShapeDtypeStruct((2, nprobe, nprobe), F32),
            jax.ShapeDtypeStruct((4, nprobe), F32),
        ),
        in_specs=[smem] * 5 + [vmem] * 3 + [hbm] * 2,
        out_specs=(vmem, vmem, vmem),
        scratch_shapes=[
            pltpu.VMEM((owned, slots, 2 * width, width), BF16),
            pltpu.VMEM(far_coupling.shape, F32),
            pltpu.VMEM((owned, 2, groups, rank, width), BF16),
            pltpu.VMEM((owned, 2, groups, rank, width), BF16),
            pltpu.VMEM((owned, 2 * width, width), BF16),
            pltpu.VMEM((2, 3 * owned + 1, rows, width), BF16),
            pltpu.VMEM((2, n, owned // per, rows, width), F32),
            pltpu.VMEM((n * owned, rows, width), F32),
            pltpu.VMEM((owned, rows, 2 * width), F32),
            field,
            field,
            field,
            field,
            field,
            pltpu.VMEM((n, nprobe, width), F32),
            pltpu.VMEM((n, rows, width), F32),
            pltpu.VMEM((n, nprobe, width), F32),
            pltpu.VMEM((n, nprobe + 2 * rows, width), F32),
            pltpu.SemaphoreType.DMA((owned,)),
            pltpu.SemaphoreType.DMA((owned,)),
            pltpu.SemaphoreType.DMA((8, n)),
            pltpu.SemaphoreType.DMA((8, n)),
        ],
        compiler_params=pltpu.CompilerParams(
            collective_id=0, has_side_effects=True, vmem_limit_bytes=52 * 2**20
        ),
    )(
        near_list,
        near_count,
        cluster_rows,
        far_list,
        weight,
        probes.reshape(owned, rows, width),
        row_basis,
        col_basis,
        near_blocks.reshape(owned, slots, 2 * width, width),
        far_coupling,
    )
    return sol.reshape(probes.shape), moment, arnoldi


def solution(mesh):
    in_specs = (
        P("clus", None, None, None),
        P(("contour", "clus"), None, None, None, None),
        P("clus", None),
        P("clus"),
        P("clus"),
        P(("contour", "clus"), None, None, None),
        P(("contour", "clus"), None, None, None),
        P("clus", None),
        P(("contour", "clus"), None, None, None, None),
        P("contour"),
    )
    out_specs = (
        P(("contour", "clus"), None, None, None),
        P("contour", None, None),
        P("contour", None),
    )
    return jax.shard_map(
        functools.partial(shards, mesh.shape["clus"]),
        mesh=mesh,
        in_specs=in_specs,
        out_specs=out_specs,
        check_vma=False,
    )
```

```python
import functools

import jax
import jax.numpy as jnp
from jax import lax
from jax.experimental import pallas as pl
from jax.experimental.pallas import tpu as pltpu
from jax.sharding import PartitionSpec as P

MESH = pl.DeviceIdType.MESH
F32 = jnp.float32
BF16 = jnp.bfloat16
BETA, PROJ, NORM, GRAM, COEF, HALO = 0, 1, 2, 3, 4, 6


def dot_nt(left, right, precision=None):
    return lax.dot_general(
        left, right, (((1,), (1,)), ((), ())), precision=precision, preferred_element_type=F32
    )


def joined(prod, half, lanes):
    re = prod[:half, :lanes] - prod[half:, lanes:]
    im = prod[half:, :lanes] + prod[:half, lanes:]
    return jnp.concatenate([re, im], axis=0)


def kernel(
    n,
    near_list,
    near_count,
    cluster_rows,
    far_list,
    weight,
    probes,
    row_basis,
    col_basis,
    near_hbm,
    far_hbm,
    solution_ref,
    moment_ref,
    arnoldi_ref,
    near_v,
    far_v,
    wide_hi,
    wide_lo,
    col_pad,
    xs,
    raw,
    spread,
    total,
    base,
    first,
    second,
    image_one,
    image_two,
    beta_s,
    proj_s,
    norm_s,
    gram_s,
    near_sem,
    far_sem,
    send_sem,
    recv_sem,
):
    owned, rows, width = probes.shape
    half = rows // 2
    slots = near_v.shape[1]
    fslots = far_v.shape[1]
    rank = far_v.shape[3]
    per = width // rank
    me = lax.axis_index("clus")

    def near_copy(i):
        return pltpu.make_async_copy(near_hbm.at[i], near_v.at[i], near_sem.at[i])

    def far_copy(i):
        return pltpu.make_async_copy(far_hbm.at[i], far_v.at[i], far_sem.at[i])

    for i in range(owned):
        far_copy(i).start()
    for i in range(owned):
        near_copy(i).start()

    barrier = pltpu.get_barrier_semaphore()
    for o in range(1, n):
        pl.semaphore_signal(
            barrier, inc=1, device_id={"clus": lax.rem(me + o, n)}, device_id_type=MESH
        )
    pl.semaphore_wait(barrier, n - 1)

    def share(buf, phase):
        def copy(slot, o):
            return pltpu.make_async_remote_copy(
                src_ref=buf.at[slot],
                dst_ref=buf.at[slot],
                send_sem=send_sem.at[phase, o],
                recv_sem=recv_sem.at[phase, o],
                device_id={"clus": lax.rem(me + o, n)},
                device_id_type=MESH,
            )

        for o in range(1, n):
            copy(me, o).start()

        def finish():
            for o in range(1, n):
                copy(lax.rem(me + n - o, n), o).wait_recv()
            for o in range(1, n):
                copy(me, o).wait_send()

        return finish

    def summed(buf):
        out = buf[0]
        for d in range(1, n):
            out = out + buf[d]
        return out

    def lane_sum(v):
        return jnp.sum(v, axis=1, keepdims=True)

    eye = lax.broadcasted_iota(jnp.int32, (half, width), 0) == lax.broadcasted_iota(
        jnp.int32, (half, width), 1
    )

    def as_row(column):
        return jnp.sum(jnp.where(eye, column, 0.0), axis=0, keepdims=True)

    def as_column(row):
        return lane_sum(jnp.where(eye, row, 0.0))

    def square_part(ref):
        acc = jnp.zeros((rows, width), F32)
        for i in range(owned):
            v = ref[i]
            acc = acc + v * v
        return acc[:half] + acc[half:]

    def inner_part(left, right):
        re = jnp.zeros((half, width), F32)
        im = jnp.zeros((half, width), F32)
        for i in range(owned):
            lr, li = left[i, :half], left[i, half:]
            rr, ri = right[i, :half], right[i, half:]
            re = re + (lr * rr + li * ri)
            im = im + (lr * ri - li * rr)
        return re, im

    lane = lax.broadcasted_iota(jnp.int32, (rows, width), 1)
    for i in range(owned):
        base[i] = jnp.where(lane < cluster_rows[i], probes[i], 0.0)
    beta_s[me] = as_row(lane_sum(square_part(base)))
    finish_beta = share(beta_s, BETA)

    col_pad[...] = jnp.zeros_like(col_pad)
    for i in range(owned):
        at = (i % per) * rank
        col_pad[i, at : at + rank] = col_basis[i, 0]
        col_pad[i, width + at : width + at + rank] = col_basis[i, 1]
    for op in range(2):
        xs[op, 3 * owned] = jnp.zeros((rows, width), BF16)

    def lay(i, carry):
        far_copy(i).wait()
        for g in range(fslots // per):
            for c in range(2):
                tile = jnp.concatenate([far_v[i, g * per + a, c] for a in range(per)], axis=1)
                hi = tile.astype(BF16)
                to = slice(c * rank, (c + 1) * rank)
                wide_hi[i, g, to] = hi
                wide_lo[i, g, to] = (tile - hi.astype(F32)).astype(BF16)
        return carry

    lax.fori_loop(0, owned, lay, 0)

    finish_beta()
    beta = jnp.sqrt(as_column(summed(beta_s)) + 1e-06)
    beta_rows = jnp.concatenate([beta, beta], axis=0)

    def operate(op, field, image, meanwhile):
        def halo(o, src, dst, to):
            return pltpu.make_async_remote_copy(
                src_ref=xs.at[op, pl.ds(src * owned, owned)],
                dst_ref=xs.at[op, pl.ds(dst * owned, owned)],
                send_sem=send_sem.at[HALO + op, o],
                recv_sem=recv_sem.at[HALO + op, o],
                device_id={"clus": to},
                device_id_type=MESH,
            )

        right, left = lax.rem(me + 1, n), lax.rem(me + n - 1, n)
        for i in range(owned):
            xs[op, owned + i] = field[i].astype(BF16)
        halo(0, 1, 0, right).start()
        halo(1, 1, 2, left).start()
        for g in range(owned // per):
            prod = jnp.zeros((rows, 2 * width), F32)
            for a in range(per):
                prod = prod + dot_nt(xs[op, owned + g * per + a], col_pad[g * per + a])
            raw[op, me, g] = joined(prod, half, width)
        finish_coef = share(raw.at[op], COEF + op)
        meanwhile()
        halo(0, 1, 0, right).wait_recv()
        halo(1, 1, 2, left).wait_recv()
        shift = (me - 1) * owned

        def near(i, carry):
            if op == 0:
                near_copy(i).wait()
            count = near_count[i]

            def pulled(k):
                at = jnp.where(k < count, near_list[i, k] - shift, 3 * owned)
                return xs[op, at]

            acc = jnp.zeros((rows, 2 * width), F32)
            for k in range(0, slots - 1, 2):
                lhs = jnp.concatenate([pulled(k), pulled(k + 1)], axis=1)
                rhs = jnp.concatenate([near_v[i, k], near_v[i, k + 1]], axis=1)
                acc = acc + dot_nt(lhs, rhs)
            if slots % 2:
                acc = acc + dot_nt(pulled(slots - 1), near_v[i, slots - 1])
            total[i] = acc
            return carry

        lax.fori_loop(0, owned, near, 0)
        finish_coef()

        def expand(d, carry):
            for g in range(owned // per):
                tile = raw[op, d, g]
                for a in range(per):
                    m = jnp.where((lane >= a * rank) & (lane < (a + 1) * rank), tile, 0.0)
                    step = width // 2
                    while step >= rank:
                        m = m + pltpu.roll(m, step, 1)
                        step //= 2
                    spread[d * owned + g * per + a] = m
            return carry

        lax.fori_loop(0, n, expand, 0)

        def far(i, carry):
            acc_hi = jnp.zeros((2 * rows, 2 * rank), F32)
            acc_lo = jnp.zeros((rows, 2 * rank), F32)

            def taken(g):
                t = spread[far_list[i, g * per]]
                for a in range(1, per):
                    t = jnp.where(lane >= a * rank, spread[far_list[i, g * per + a]], t)
                hi = t.astype(BF16)
                lo = (t - hi.astype(F32)).astype(BF16)
                return jnp.concatenate([hi, lo], axis=0)

            for g in range(0, fslots // per, 2):
                both = jnp.concatenate([taken(g), taken(g + 1)], axis=1)
                w_hi = jnp.concatenate([wide_hi[i, g], wide_hi[i, g + 1]], axis=1)
                w_lo = jnp.concatenate([wide_lo[i, g], wide_lo[i, g + 1]], axis=1)
                acc_hi = acc_hi + dot_nt(both, w_hi)
                acc_lo = acc_lo + dot_nt(both[:rows], w_lo)
            acc = acc_hi[:rows] + (acc_hi[rows:] + acc_lo)
            acc_r, acc_i = acc[:, :rank], acc[:, rank:]
            fr = acc_r[:half] - acc_i[half:]
            fi = acc_r[half:] + acc_i[:half]
            coef = jnp.concatenate([fr, fi], axis=0).astype(BF16)
            basis = jnp.concatenate([row_basis[i, 0], row_basis[i, 1]], axis=1)
            prod = total[i] + jnp.dot(coef, basis, preferred_element_type=F32)
            image[i] = jnp.where(lane < cluster_rows[i], joined(prod, half, width), 0.0)
            return carry

        lax.fori_loop(0, owned, far, 0)
        halo(0, 1, 0, right).wait_send()
        halo(1, 1, 2, left).wait_send()

    for i in range(owned):
        first[i] = base[i] / beta_rows
    operate(0, first, image_one, lambda: None)

    re, im = inner_part(first, image_one)
    proj_s[me, 0:1] = as_row(lane_sum(re))
    proj_s[me, 1:2] = as_row(lane_sum(im))
    share(proj_s, PROJ)()
    proj = summed(proj_s)
    pr, pi = as_column(proj[0:1]), as_column(proj[1:2])
    for i in range(owned):
        fr, fi = first[i, :half], first[i, half:]
        second[i, :half] = image_one[i, :half] - (pr * fr - pi * fi)
        second[i, half:] = image_one[i, half:] - (pr * fi + pi * fr)
    norm_s[me] = as_row(lane_sum(square_part(second)))
    share(norm_s, NORM)()
    size_two = jnp.sqrt(as_column(summed(norm_s)) + 1e-06)
    size_rows = jnp.concatenate([size_two, size_two], axis=0)
    for i in range(owned):
        second[i] = second[i] / size_rows

    def moments():
        m1 = jnp.zeros((rows, rows), F32)
        m2 = jnp.zeros((rows, rows), F32)
        for i in range(owned):
            m1 = m1 + dot_nt(base[i], first[i], lax.Precision.HIGHEST)
            m2 = m2 + dot_nt(base[i], second[i], lax.Precision.HIGHEST)
        gram_s[me] = jnp.zeros(gram_s.shape[1:], F32)
        for at, m in ((0, m1), (rows, m2)):
            re = m[:half, :half] + m[half:, half:]
            im = m[:half, half:] - m[half:, :half]
            gram_s[me, :, at : at + rows] = jnp.concatenate([re, im], axis=1)

    operate(1, second, image_two, moments)

    parts = (
        square_part(image_one),
        square_part(image_two),
        *inner_part(image_one, image_two),
        *inner_part(image_one, base),
        *inner_part(image_two, base),
    )
    narrow = lax.broadcasted_iota(jnp.int32, (half, width), 1)
    packed = gram_s[me]
    for k, part in enumerate(parts):
        packed = jnp.where(narrow == 2 * rows + k, lane_sum(part), packed)
    gram_s[me] = packed
    share(gram_s, GRAM)()
    gram = summed(gram_s)
    g11, g22, g12r, g12i, q1r, q1i, q2r, q2i = (
        lane_sum(jnp.where(narrow == 2 * rows + k, gram, 0.0)) for k in range(8)
    )
    det = g11 * g22 - (g12r * g12r + g12i * g12i)
    y1r = (g22 * q1r - (g12r * q2r - g12i * q2i)) / det
    y1i = (g22 * q1i - (g12r * q2i + g12i * q2r)) / det
    y2r = (g11 * q2r - (g12r * q1r + g12i * q1i)) / det
    y2i = (g11 * q2i - (g12r * q1i - g12i * q1r)) / det
    wr, wi = weight[0], weight[1]
    y1r, y1i = wr * y1r - wi * y1i, wr * y1i + wi * y1r
    y2r, y2i = wr * y2r - wi * y2i, wr * y2i + wi * y2r
    for i in range(owned):
        fr, fi = first[i, :half], first[i, half:]
        sr, si = second[i, :half], second[i, half:]
        solution_ref[i, :half] = (y1r * fr - y1i * fi) + (y2r * sr - y2i * si)
        solution_ref[i, half:] = (y1r * fi + y1i * fr) + (y2r * si + y2i * sr)

    factor = 1.0 / (n * owned * width)
    arnoldi_ref[0:1] = as_row(beta * jnp.sqrt(F32(factor)))[:, :half]
    arnoldi_ref[1:2] = as_row(pr)[:, :half]
    arnoldi_ref[2:3] = as_row(pi)[:, :half]
    arnoldi_ref[3:4] = as_row(size_two)[:, :half]

    m1r, m1i, m2r, m2i = (gram[:, k * half : (k + 1) * half] for k in range(4))
    y1r, y1i, y2r, y2i = (as_row(y)[:, :half] for y in (y1r, y1i, y2r, y2i))
    moment_ref[0] = ((y1r * m1r - y1i * m1i) + (y2r * m2r - y2i * m2i)) * factor
    moment_ref[1] = ((y1r * m1i + y1i * m1r) + (y2r * m2i + y2i * m2r)) * factor


def shards(
    n,
    probes,
    near_blocks,
    near_list,
    near_count,
    cluster_rows,
    row_basis,
    col_basis,
    far_list,
    far_coupling,
    weight,
):
    owned, _, nprobe, width = probes.shape
    rows = 2 * nprobe
    slots = near_blocks.shape[1]
    fslots = far_coupling.shape[1]
    rank = far_coupling.shape[3]
    per = width // rank
    groups = fslots // per
    smem = pl.BlockSpec(memory_space=pltpu.SMEM)
    vmem = pl.BlockSpec(memory_space=pltpu.VMEM)
    hbm = pl.BlockSpec(memory_space=pl.ANY)
    field = pltpu.VMEM((owned, rows, width), F32)
    sol, moment, arnoldi = pl.pallas_call(
        functools.partial(kernel, n),
        out_shape=(
            jax.ShapeDtypeStruct((owned, rows, width), F32),
            jax.ShapeDtypeStruct((2, nprobe, nprobe), F32),
            jax.ShapeDtypeStruct((4, nprobe), F32),
        ),
        in_specs=[smem] * 5 + [vmem] * 3 + [hbm] * 2,
        out_specs=(vmem, vmem, vmem),
        scratch_shapes=[
            pltpu.VMEM((owned, slots, 2 * width, width), BF16),
            pltpu.VMEM(far_coupling.shape, F32),
            pltpu.VMEM((owned, groups, 2 * rank, width), BF16),
            pltpu.VMEM((owned, groups, 2 * rank, width), BF16),
            pltpu.VMEM((owned, 2 * width, width), BF16),
            pltpu.VMEM((2, 3 * owned + 1, rows, width), BF16),
            pltpu.VMEM((2, n, owned // per, rows, width), F32),
            pltpu.VMEM((n * owned, rows, width), F32),
            pltpu.VMEM((owned, rows, 2 * width), F32),
            field,
            field,
            field,
            field,
            field,
            pltpu.VMEM((n, 1, width), F32),
            pltpu.VMEM((n, 2, width), F32),
            pltpu.VMEM((n, 1, width), F32),
            pltpu.VMEM((n, nprobe, width), F32),
            pltpu.SemaphoreType.DMA((owned,)),
            pltpu.SemaphoreType.DMA((owned,)),
            pltpu.SemaphoreType.DMA((8, n)),
            pltpu.SemaphoreType.DMA((8, n)),
        ],
        compiler_params=pltpu.CompilerParams(
            collective_id=0, has_side_effects=True, vmem_limit_bytes=60 * 2**20
        ),
    )(
        near_list,
        near_count,
        cluster_rows,
        far_list,
        weight,
        probes.reshape(owned, rows, width),
        row_basis,
        col_basis,
        near_blocks.reshape(owned, slots, 2 * width, width),
        far_coupling,
    )
    return sol.reshape(probes.shape), moment, arnoldi


def solution(mesh):
    in_specs = (
        P("clus", None, None, None),
        P(("contour", "clus"), None, None, None, None),
        P("clus", None),
        P("clus"),
        P("clus"),
        P(("contour", "clus"), None, None, None),
        P(("contour", "clus"), None, None, None),
        P("clus", None),
        P(("contour", "clus"), None, None, None, None),
        P("contour"),
    )
    out_specs = (
        P(("contour", "clus"), None, None, None),
        P("contour", None, None),
        P("contour", None),
    )
    return jax.shard_map(
        functools.partial(shards, mesh.shape["clus"]),
        mesh=mesh,
        in_specs=in_specs,
        out_specs=out_specs,
        check_vma=False,
    )
```

```python
import functools

import jax
import jax.numpy as jnp
from jax import lax
from jax.experimental import pallas as pl
from jax.experimental.pallas import tpu as pltpu
from jax.sharding import PartitionSpec as P

MESH = pl.DeviceIdType.MESH
F32 = jnp.float32
BF16 = jnp.bfloat16
BETA, PROJ, NORM, GRAM, COEF, HALO = 0, 1, 2, 3, 4, 6


def dot_nt(left, right, precision=None):
    return lax.dot_general(
        left, right, (((1,), (1,)), ((), ())), precision=precision, preferred_element_type=F32
    )


def joined(prod, half, lanes):
    re = prod[:half, :lanes] - prod[half:, lanes:]
    im = prod[half:, :lanes] + prod[:half, lanes:]
    return jnp.concatenate([re, im], axis=0)


def kernel(
    n,
    near_list,
    near_count,
    cluster_rows,
    far_list,
    weight,
    probes,
    row_basis,
    col_basis,
    near_hbm,
    far_hbm,
    solution_ref,
    moment_ref,
    arnoldi_ref,
    near_v,
    far_v,
    wide_hi,
    wide_lo,
    col_pad,
    xs,
    raw,
    spread,
    total,
    base,
    first,
    second,
    image_one,
    image_two,
    beta_s,
    proj_s,
    norm_s,
    gram_s,
    near_sem,
    far_sem,
    send_sem,
    recv_sem,
):
    owned, rows, width = probes.shape
    half = rows // 2
    slots = near_v.shape[1]
    fslots = far_v.shape[1]
    rank = far_v.shape[3]
    per = width // rank
    me = lax.axis_index("clus")

    def near_copy(i):
        return pltpu.make_async_copy(near_hbm.at[i], near_v.at[i], near_sem.at[i])

    def far_copy(i):
        return pltpu.make_async_copy(far_hbm.at[i], far_v.at[i], far_sem.at[i])

    for i in range(owned):
        far_copy(i).start()
    for i in range(owned):
        near_copy(i).start()

    barrier = pltpu.get_barrier_semaphore()
    for o in range(1, n):
        pl.semaphore_signal(
            barrier, inc=1, device_id={"clus": lax.rem(me + o, n)}, device_id_type=MESH
        )
    pl.semaphore_wait(barrier, n - 1)

    def share(buf, phase):
        def copy(slot, o):
            return pltpu.make_async_remote_copy(
                src_ref=buf.at[slot],
                dst_ref=buf.at[slot],
                send_sem=send_sem.at[phase, o],
                recv_sem=recv_sem.at[phase, o],
                device_id={"clus": lax.rem(me + o, n)},
                device_id_type=MESH,
            )

        for o in range(1, n):
            copy(me, o).start()

        def finish():
            for o in range(1, n):
                copy(lax.rem(me + n - o, n), o).wait_recv()
            for o in range(1, n):
                copy(me, o).wait_send()

        return finish

    def summed(buf):
        out = buf[0]
        for d in range(1, n):
            out = out + buf[d]
        return out

    def lane_sum(v):
        return jnp.sum(v, axis=1, keepdims=True)

    eye = lax.broadcasted_iota(jnp.int32, (half, width), 0) == lax.broadcasted_iota(
        jnp.int32, (half, width), 1
    )

    def as_row(column):
        return jnp.sum(jnp.where(eye, column, 0.0), axis=0, keepdims=True)

    def as_column(row):
        return lane_sum(jnp.where(eye, row, 0.0))

    def square_part(ref):
        acc = jnp.zeros((rows, width), F32)
        for i in range(owned):
            v = ref[i]
            acc = acc + v * v
        return acc[:half] + acc[half:]

    def inner_part(left, right):
        re = jnp.zeros((half, width), F32)
        im = jnp.zeros((half, width), F32)
        for i in range(owned):
            lr, li = left[i, :half], left[i, half:]
            rr, ri = right[i, :half], right[i, half:]
            re = re + (lr * rr + li * ri)
            im = im + (lr * ri - li * rr)
        return re, im

    lane = lax.broadcasted_iota(jnp.int32, (rows, width), 1)
    for i in range(owned):
        base[i] = jnp.where(lane < cluster_rows[i], probes[i], 0.0)
    beta_s[me] = as_row(lane_sum(square_part(base)))
    finish_beta = share(beta_s, BETA)

    col_pad[...] = jnp.zeros_like(col_pad)
    for i in range(owned):
        at = (i % per) * rank
        col_pad[i, at : at + rank] = col_basis[i, 0]
        col_pad[i, width + at : width + at + rank] = col_basis[i, 1]
    for op in range(2):
        xs[op, 3 * owned] = jnp.zeros((rows, width), BF16)

    def lay(i, carry):
        far_copy(i).wait()
        for g in range(fslots // per):
            for c in range(2):
                tile = jnp.concatenate([far_v[i, g * per + a, c] for a in range(per)], axis=1)
                hi = tile.astype(BF16)
                to = slice(c * rank, (c + 1) * rank)
                wide_hi[i, g, to] = hi
                wide_lo[i, g, to] = (tile - hi.astype(F32)).astype(BF16)
        return carry

    lax.fori_loop(0, owned, lay, 0)

    finish_beta()
    beta = jnp.sqrt(as_column(summed(beta_s)) + 1e-06)
    beta_rows = jnp.concatenate([beta, beta], axis=0)

    def operate(op, field, image, meanwhile):
        def halo(o, src, dst, to):
            return pltpu.make_async_remote_copy(
                src_ref=xs.at[op, pl.ds(src * owned, owned)],
                dst_ref=xs.at[op, pl.ds(dst * owned, owned)],
                send_sem=send_sem.at[HALO + op, o],
                recv_sem=recv_sem.at[HALO + op, o],
                device_id={"clus": to},
                device_id_type=MESH,
            )

        right, left = lax.rem(me + 1, n), lax.rem(me + n - 1, n)
        for i in range(owned):
            xs[op, owned + i] = field[i].astype(BF16)
        halo(0, 1, 0, right).start()
        halo(1, 1, 2, left).start()
        for g in range(owned // per):
            prod = jnp.zeros((rows, 2 * width), F32)
            for a in range(per):
                prod = prod + dot_nt(xs[op, owned + g * per + a], col_pad[g * per + a])
            raw[op, me, g] = joined(prod, half, width)
        finish_coef = share(raw.at[op], COEF + op)
        meanwhile()
        halo(0, 1, 0, right).wait_recv()
        halo(1, 1, 2, left).wait_recv()
        shift = (me - 1) * owned

        def near(i, carry):
            if op == 0:
                near_copy(i).wait()
            count = near_count[i]

            def pulled(k):
                at = jnp.where(k < count, near_list[i, k] - shift, 3 * owned)
                return xs[op, at]

            acc = jnp.zeros((rows, 2 * width), F32)
            for k in range(0, slots - 1, 2):
                lhs = jnp.concatenate([pulled(k), pulled(k + 1)], axis=1)
                rhs = jnp.concatenate([near_v[i, k], near_v[i, k + 1]], axis=1)
                acc = acc + dot_nt(lhs, rhs)
            if slots % 2:
                acc = acc + dot_nt(pulled(slots - 1), near_v[i, slots - 1])
            total[i] = acc
            return carry

        lax.fori_loop(0, owned, near, 0, unroll=2)
        finish_coef()

        def expand(d, carry):
            for g in range(owned // per):
                tile = raw[op, d, g]
                for a in range(per):
                    m = jnp.where((lane >= a * rank) & (lane < (a + 1) * rank), tile, 0.0)
                    step = width // 2
                    while step >= rank:
                        m = m + pltpu.roll(m, step, 1)
                        step //= 2
                    spread[d * owned + g * per + a] = m
            return carry

        lax.fori_loop(0, n, expand, 0, unroll=4)

        def far(i, carry):
            acc_hi = jnp.zeros((2 * rows, 2 * rank), F32)
            acc_lo = jnp.zeros((rows, 2 * rank), F32)

            def taken(g):
                t = spread[far_list[i, g * per]]
                for a in range(1, per):
                    t = jnp.where(lane >= a * rank, spread[far_list[i, g * per + a]], t)
                hi = t.astype(BF16)
                lo = (t - hi.astype(F32)).astype(BF16)
                return jnp.concatenate([hi, lo], axis=0)

            for g in range(0, fslots // per, 2):
                both = jnp.concatenate([taken(g), taken(g + 1)], axis=1)
                w_hi = jnp.concatenate([wide_hi[i, g], wide_hi[i, g + 1]], axis=1)
                w_lo = jnp.concatenate([wide_lo[i, g], wide_lo[i, g + 1]], axis=1)
                acc_hi = acc_hi + dot_nt(both, w_hi)
                acc_lo = acc_lo + dot_nt(both[:rows], w_lo)
            acc = acc_hi[:rows] + (acc_hi[rows:] + acc_lo)
            acc_r, acc_i = acc[:, :rank], acc[:, rank:]
            fr = acc_r[:half] - acc_i[half:]
            fi = acc_r[half:] + acc_i[:half]
            coef = jnp.concatenate([fr, fi], axis=0).astype(BF16)
            basis = jnp.concatenate([row_basis[i, 0], row_basis[i, 1]], axis=1)
            prod = total[i] + jnp.dot(coef, basis, preferred_element_type=F32)
            image[i] = jnp.where(lane < cluster_rows[i], joined(prod, half, width), 0.0)
            return carry

        lax.fori_loop(0, owned, far, 0, unroll=4)
        halo(0, 1, 0, right).wait_send()
        halo(1, 1, 2, left).wait_send()

    for i in range(owned):
        first[i] = base[i] / beta_rows
    operate(0, first, image_one, lambda: None)

    re, im = inner_part(first, image_one)
    proj_s[me, 0:1] = as_row(lane_sum(re))
    proj_s[me, 1:2] = as_row(lane_sum(im))
    share(proj_s, PROJ)()
    proj = summed(proj_s)
    pr, pi = as_column(proj[0:1]), as_column(proj[1:2])
    for i in range(owned):
        fr, fi = first[i, :half], first[i, half:]
        second[i, :half] = image_one[i, :half] - (pr * fr - pi * fi)
        second[i, half:] = image_one[i, half:] - (pr * fi + pi * fr)
    norm_s[me] = as_row(lane_sum(square_part(second)))
    share(norm_s, NORM)()
    size_two = jnp.sqrt(as_column(summed(norm_s)) + 1e-06)
    size_rows = jnp.concatenate([size_two, size_two], axis=0)
    for i in range(owned):
        second[i] = second[i] / size_rows

    def moments():
        m1 = jnp.zeros((rows, rows), F32)
        m2 = jnp.zeros((rows, rows), F32)
        for i in range(owned):
            m1 = m1 + dot_nt(base[i], first[i], lax.Precision.HIGHEST)
            m2 = m2 + dot_nt(base[i], second[i], lax.Precision.HIGHEST)
        gram_s[me] = jnp.zeros(gram_s.shape[1:], F32)
        for at, m in ((0, m1), (rows, m2)):
            re = m[:half, :half] + m[half:, half:]
            im = m[:half, half:] - m[half:, :half]
            gram_s[me, :, at : at + rows] = jnp.concatenate([re, im], axis=1)

    operate(1, second, image_two, moments)

    parts = (
        square_part(image_one),
        square_part(image_two),
        *inner_part(image_one, image_two),
        *inner_part(image_one, base),
        *inner_part(image_two, base),
    )
    narrow = lax.broadcasted_iota(jnp.int32, (half, width), 1)
    packed = gram_s[me]
    for k, part in enumerate(parts):
        packed = jnp.where(narrow == 2 * rows + k, lane_sum(part), packed)
    gram_s[me] = packed
    share(gram_s, GRAM)()
    gram = summed(gram_s)
    g11, g22, g12r, g12i, q1r, q1i, q2r, q2i = (
        lane_sum(jnp.where(narrow == 2 * rows + k, gram, 0.0)) for k in range(8)
    )
    det = g11 * g22 - (g12r * g12r + g12i * g12i)
    y1r = (g22 * q1r - (g12r * q2r - g12i * q2i)) / det
    y1i = (g22 * q1i - (g12r * q2i + g12i * q2r)) / det
    y2r = (g11 * q2r - (g12r * q1r + g12i * q1i)) / det
    y2i = (g11 * q2i - (g12r * q1i - g12i * q1r)) / det
    wr, wi = weight[0], weight[1]
    y1r, y1i = wr * y1r - wi * y1i, wr * y1i + wi * y1r
    y2r, y2i = wr * y2r - wi * y2i, wr * y2i + wi * y2r
    for i in range(owned):
        fr, fi = first[i, :half], first[i, half:]
        sr, si = second[i, :half], second[i, half:]
        solution_ref[i, :half] = (y1r * fr - y1i * fi) + (y2r * sr - y2i * si)
        solution_ref[i, half:] = (y1r * fi + y1i * fr) + (y2r * si + y2i * sr)

    factor = 1.0 / (n * owned * width)
    arnoldi_ref[0:1] = as_row(beta * jnp.sqrt(F32(factor)))[:, :half]
    arnoldi_ref[1:2] = as_row(pr)[:, :half]
    arnoldi_ref[2:3] = as_row(pi)[:, :half]
    arnoldi_ref[3:4] = as_row(size_two)[:, :half]

    m1r, m1i, m2r, m2i = (gram[:, k * half : (k + 1) * half] for k in range(4))
    y1r, y1i, y2r, y2i = (as_row(y)[:, :half] for y in (y1r, y1i, y2r, y2i))
    moment_ref[0] = ((y1r * m1r - y1i * m1i) + (y2r * m2r - y2i * m2i)) * factor
    moment_ref[1] = ((y1r * m1i + y1i * m1r) + (y2r * m2i + y2i * m2r)) * factor


def shards(
    n,
    probes,
    near_blocks,
    near_list,
    near_count,
    cluster_rows,
    row_basis,
    col_basis,
    far_list,
    far_coupling,
    weight,
):
    owned, _, nprobe, width = probes.shape
    rows = 2 * nprobe
    slots = near_blocks.shape[1]
    fslots = far_coupling.shape[1]
    rank = far_coupling.shape[3]
    per = width // rank
    groups = fslots // per
    smem = pl.BlockSpec(memory_space=pltpu.SMEM)
    vmem = pl.BlockSpec(memory_space=pltpu.VMEM)
    hbm = pl.BlockSpec(memory_space=pl.ANY)
    field = pltpu.VMEM((owned, rows, width), F32)
    sol, moment, arnoldi = pl.pallas_call(
        functools.partial(kernel, n),
        out_shape=(
            jax.ShapeDtypeStruct((owned, rows, width), F32),
            jax.ShapeDtypeStruct((2, nprobe, nprobe), F32),
            jax.ShapeDtypeStruct((4, nprobe), F32),
        ),
        in_specs=[smem] * 5 + [vmem] * 3 + [hbm] * 2,
        out_specs=(vmem, vmem, vmem),
        scratch_shapes=[
            pltpu.VMEM((owned, slots, 2 * width, width), BF16),
            pltpu.VMEM(far_coupling.shape, F32),
            pltpu.VMEM((owned, groups, 2 * rank, width), BF16),
            pltpu.VMEM((owned, groups, 2 * rank, width), BF16),
            pltpu.VMEM((owned, 2 * width, width), BF16),
            pltpu.VMEM((2, 3 * owned + 1, rows, width), BF16),
            pltpu.VMEM((2, n, owned // per, rows, width), F32),
            pltpu.VMEM((n * owned, rows, width), F32),
            pltpu.VMEM((owned, rows, 2 * width), F32),
            field,
            field,
            field,
            field,
            field,
            pltpu.VMEM((n, 1, width), F32),
            pltpu.VMEM((n, 2, width), F32),
            pltpu.VMEM((n, 1, width), F32),
            pltpu.VMEM((n, nprobe, width), F32),
            pltpu.SemaphoreType.DMA((owned,)),
            pltpu.SemaphoreType.DMA((owned,)),
            pltpu.SemaphoreType.DMA((8, n)),
            pltpu.SemaphoreType.DMA((8, n)),
        ],
        compiler_params=pltpu.CompilerParams(
            collective_id=0, has_side_effects=True, vmem_limit_bytes=60 * 2**20
        ),
    )(
        near_list,
        near_count,
        cluster_rows,
        far_list,
        weight,
        probes.reshape(owned, rows, width),
        row_basis,
        col_basis,
        near_blocks.reshape(owned, slots, 2 * width, width),
        far_coupling,
    )
    return sol.reshape(probes.shape), moment, arnoldi


def solution(mesh):
    in_specs = (
        P("clus", None, None, None),
        P(("contour", "clus"), None, None, None, None),
        P("clus", None),
        P("clus"),
        P("clus"),
        P(("contour", "clus"), None, None, None),
        P(("contour", "clus"), None, None, None),
        P("clus", None),
        P(("contour", "clus"), None, None, None, None),
        P("contour"),
    )
    out_specs = (
        P(("contour", "clus"), None, None, None),
        P("contour", None, None),
        P("contour", None),
    )
    return jax.shard_map(
        functools.partial(shards, mesh.shape["clus"]),
        mesh=mesh,
        in_specs=in_specs,
        out_specs=out_specs,
        check_vma=False,
    )
```

```python
import functools

import jax
import jax.numpy as jnp
from jax import lax
from jax.experimental import pallas as pl
from jax.experimental.pallas import tpu as pltpu
from jax.sharding import PartitionSpec as P

MESH = pl.DeviceIdType.MESH
F32 = jnp.float32
BF16 = jnp.bfloat16
BETA, PROJ, NORM, GRAM, COEF, HALO = 0, 1, 2, 3, 4, 6


def dot_nt(left, right, precision=None):
    return lax.dot_general(
        left, right, (((1,), (1,)), ((), ())), precision=precision, preferred_element_type=F32
    )


def joined(prod, half, lanes):
    re = prod[:half, :lanes] - prod[half:, lanes:]
    im = prod[half:, :lanes] + prod[:half, lanes:]
    return jnp.concatenate([re, im], axis=0)


def kernel(
    n,
    near_list,
    near_count,
    cluster_rows,
    far_list,
    weight,
    probes,
    row_basis,
    col_basis,
    near_hbm,
    far_hbm,
    solution_ref,
    moment_ref,
    arnoldi_ref,
    near_v,
    far_v,
    wide_hi,
    wide_lo,
    col_pad,
    xs,
    raw,
    spread,
    total,
    base,
    first,
    second,
    image_one,
    image_two,
    beta_s,
    proj_s,
    norm_s,
    gram_s,
    near_sem,
    far_sem,
    send_sem,
    recv_sem,
):
    owned, rows, width = probes.shape
    half = rows // 2
    slots = near_v.shape[1]
    fslots = far_v.shape[1]
    rank = far_v.shape[3]
    per = width // rank
    me = lax.axis_index("clus")

    def near_copy(i):
        return pltpu.make_async_copy(near_hbm.at[i], near_v.at[i], near_sem.at[i])

    def far_copy(i):
        return pltpu.make_async_copy(far_hbm.at[i], far_v.at[i], far_sem.at[i])

    for i in range(owned):
        far_copy(i).start()
    for i in range(owned):
        near_copy(i).start()

    barrier = pltpu.get_barrier_semaphore()
    for o in range(1, n):
        pl.semaphore_signal(
            barrier, inc=1, device_id={"clus": lax.rem(me + o, n)}, device_id_type=MESH
        )
    pl.semaphore_wait(barrier, n - 1)

    def share(buf, phase):
        def copy(slot, o):
            return pltpu.make_async_remote_copy(
                src_ref=buf.at[slot],
                dst_ref=buf.at[slot],
                send_sem=send_sem.at[phase, o],
                recv_sem=recv_sem.at[phase, o],
                device_id={"clus": lax.rem(me + o, n)},
                device_id_type=MESH,
            )

        for o in range(1, n):
            copy(me, o).start()

        def finish():
            for o in range(1, n):
                copy(lax.rem(me + n - o, n), o).wait_recv()
            for o in range(1, n):
                copy(me, o).wait_send()

        return finish

    def summed(buf):
        out = buf[0]
        for d in range(1, n):
            out = out + buf[d]
        return out

    def lane_sum(v):
        return jnp.sum(v, axis=1, keepdims=True)

    eye = lax.broadcasted_iota(jnp.int32, (half, width), 0) == lax.broadcasted_iota(
        jnp.int32, (half, width), 1
    )

    def as_row(column):
        return jnp.sum(jnp.where(eye, column, 0.0), axis=0, keepdims=True)

    def as_column(row):
        return lane_sum(jnp.where(eye, row, 0.0))

    def square_part(ref):
        acc = jnp.zeros((rows, width), F32)
        for i in range(owned):
            v = ref[i]
            acc = acc + v * v
        return acc[:half] + acc[half:]

    def inner_part(left, right):
        re = jnp.zeros((half, width), F32)
        im = jnp.zeros((half, width), F32)
        for i in range(owned):
            lr, li = left[i, :half], left[i, half:]
            rr, ri = right[i, :half], right[i, half:]
            re = re + (lr * rr + li * ri)
            im = im + (lr * ri - li * rr)
        return re, im

    lane = lax.broadcasted_iota(jnp.int32, (rows, width), 1)
    for i in range(owned):
        base[i] = jnp.where(lane < cluster_rows[i], probes[i], 0.0)
    beta_s[me] = as_row(lane_sum(square_part(base)))
    finish_beta = share(beta_s, BETA)

    col_pad[...] = jnp.zeros_like(col_pad)
    for i in range(owned):
        at = (i % per) * rank
        col_pad[i, at : at + rank] = col_basis[i, 0]
        col_pad[i, width + at : width + at + rank] = col_basis[i, 1]
    for op in range(2):
        xs[op, 3 * owned] = jnp.zeros((rows, width), BF16)

    def lay(i, carry):
        far_copy(i).wait()
        for g in range(fslots // per):
            for c in range(2):
                tile = jnp.concatenate([far_v[i, g * per + a, c] for a in range(per)], axis=1)
                hi = tile.astype(BF16)
                to = slice(c * rank, (c + 1) * rank)
                wide_hi[i, g, to] = hi
                wide_lo[i, g, to] = (tile - hi.astype(F32)).astype(BF16)
        return carry

    lax.fori_loop(0, owned, lay, 0)

    finish_beta()
    beta = jnp.sqrt(as_column(summed(beta_s)) + 1e-06)
    beta_rows = jnp.concatenate([beta, beta], axis=0)

    def operate(op, field, image, meanwhile):
        def halo(o, src, dst, to):
            return pltpu.make_async_remote_copy(
                src_ref=xs.at[op, pl.ds(src * owned, owned)],
                dst_ref=xs.at[op, pl.ds(dst * owned, owned)],
                send_sem=send_sem.at[HALO + op, o],
                recv_sem=recv_sem.at[HALO + op, o],
                device_id={"clus": to},
                device_id_type=MESH,
            )

        right, left = lax.rem(me + 1, n), lax.rem(me + n - 1, n)
        for i in range(owned):
            xs[op, owned + i] = field[i].astype(BF16)
        halo(0, 1, 0, right).start()
        halo(1, 1, 2, left).start()
        for g in range(owned // per):
            prod = jnp.zeros((rows, 2 * width), F32)
            for a in range(per):
                prod = prod + dot_nt(xs[op, owned + g * per + a], col_pad[g * per + a])
            raw[op, me, g] = joined(prod, half, width)
        finish_coef = share(raw.at[op], COEF + op)
        meanwhile()
        halo(0, 1, 0, right).wait_recv()
        halo(1, 1, 2, left).wait_recv()
        shift = (me - 1) * owned

        def near(i, carry):
            if op == 0:
                near_copy(i).wait()
            count = near_count[i]

            def pulled(k):
                at = jnp.where(k < count, near_list[i, k] - shift, 3 * owned)
                return xs[op, at]

            acc = jnp.zeros((rows, 2 * width), F32)
            for k in range(0, slots - 1, 2):
                lhs = jnp.concatenate([pulled(k), pulled(k + 1)], axis=1)
                rhs = jnp.concatenate([near_v[i, k], near_v[i, k + 1]], axis=1)
                acc = acc + dot_nt(lhs, rhs)
            if slots % 2:
                acc = acc + dot_nt(pulled(slots - 1), near_v[i, slots - 1])
            total[i] = acc
            return carry

        lax.fori_loop(0, owned, near, 0)
        finish_coef()

        def expand(d, carry):
            for g in range(owned // per):
                tile = raw[op, d, g]
                for a in range(per):
                    m = jnp.where((lane >= a * rank) & (lane < (a + 1) * rank), tile, 0.0)
                    step = width // 2
                    while step >= rank:
                        m = m + pltpu.roll(m, step, 1)
                        step //= 2
                    spread[d * owned + g * per + a] = m
            return carry

        lax.fori_loop(0, n, expand, 0)

        def far(i, carry):
            acc_hi = jnp.zeros((2 * rows, 2 * rank), F32)
            acc_lo = jnp.zeros((rows, 2 * rank), F32)

            def taken(g):
                t = spread[far_list[i, g * per]]
                for a in range(1, per):
                    t = jnp.where(lane >= a * rank, spread[far_list[i, g * per + a]], t)
                hi = t.astype(BF16)
                lo = (t - hi.astype(F32)).astype(BF16)
                return jnp.concatenate([hi, lo], axis=0)

            for g in range(0, fslots // per, 2):
                both = jnp.concatenate([taken(g), taken(g + 1)], axis=1)
                w_hi = jnp.concatenate([wide_hi[i, g], wide_hi[i, g + 1]], axis=1)
                w_lo = jnp.concatenate([wide_lo[i, g], wide_lo[i, g + 1]], axis=1)
                acc_hi = acc_hi + dot_nt(both, w_hi)
                acc_lo = acc_lo + dot_nt(both[:rows], w_lo)
            acc = acc_hi[:rows] + (acc_hi[rows:] + acc_lo)
            acc_r, acc_i = acc[:, :rank], acc[:, rank:]
            fr = acc_r[:half] - acc_i[half:]
            fi = acc_r[half:] + acc_i[:half]
            coef = jnp.concatenate([fr, fi], axis=0).astype(BF16)
            basis = jnp.concatenate([row_basis[i, 0], row_basis[i, 1]], axis=1)
            prod = total[i] + jnp.dot(coef, basis, preferred_element_type=F32)
            image[i] = jnp.where(lane < cluster_rows[i], joined(prod, half, width), 0.0)
            return carry

        lax.fori_loop(0, owned, far, 0)
        halo(0, 1, 0, right).wait_send()
        halo(1, 1, 2, left).wait_send()

    for i in range(owned):
        first[i] = base[i] / beta_rows
    operate(0, first, image_one, lambda: None)

    re, im = inner_part(first, image_one)
    proj_s[me, 0:1] = as_row(lane_sum(re))
    proj_s[me, 1:2] = as_row(lane_sum(im))
    share(proj_s, PROJ)()
    proj = summed(proj_s)
    pr, pi = as_column(proj[0:1]), as_column(proj[1:2])
    for i in range(owned):
        fr, fi = first[i, :half], first[i, half:]
        second[i, :half] = image_one[i, :half] - (pr * fr - pi * fi)
        second[i, half:] = image_one[i, half:] - (pr * fi + pi * fr)
    norm_s[me] = as_row(lane_sum(square_part(second)))
    share(norm_s, NORM)()
    size_two = jnp.sqrt(as_column(summed(norm_s)) + 1e-06)
    size_rows = jnp.concatenate([size_two, size_two], axis=0)
    for i in range(owned):
        second[i] = second[i] / size_rows

    def moments():
        left = jnp.concatenate([base[i] for i in range(owned)], axis=1)
        right = jnp.concatenate(
            [jnp.concatenate([first[i], second[i]], axis=0) for i in range(owned)], axis=1
        )
        m = dot_nt(left, right, lax.Precision.HIGHEST)
        m1, m2 = m[:, :rows], m[:, rows:]
        gram_s[me] = jnp.zeros(gram_s.shape[1:], F32)
        for at, m in ((0, m1), (rows, m2)):
            re = m[:half, :half] + m[half:, half:]
            im = m[:half, half:] - m[half:, :half]
            gram_s[me, :, at : at + rows] = jnp.concatenate([re, im], axis=1)

    operate(1, second, image_two, moments)

    parts = (
        square_part(image_one),
        square_part(image_two),
        *inner_part(image_one, image_two),
        *inner_part(image_one, base),
        *inner_part(image_two, base),
    )
    narrow = lax.broadcasted_iota(jnp.int32, (half, width), 1)
    packed = gram_s[me]
    for k, part in enumerate(parts):
        packed = jnp.where(narrow == 2 * rows + k, lane_sum(part), packed)
    gram_s[me] = packed
    share(gram_s, GRAM)()
    gram = summed(gram_s)
    g11, g22, g12r, g12i, q1r, q1i, q2r, q2i = (
        lane_sum(jnp.where(narrow == 2 * rows + k, gram, 0.0)) for k in range(8)
    )
    det = g11 * g22 - (g12r * g12r + g12i * g12i)
    y1r = (g22 * q1r - (g12r * q2r - g12i * q2i)) / det
    y1i = (g22 * q1i - (g12r * q2i + g12i * q2r)) / det
    y2r = (g11 * q2r - (g12r * q1r + g12i * q1i)) / det
    y2i = (g11 * q2i - (g12r * q1i - g12i * q1r)) / det
    wr, wi = weight[0], weight[1]
    y1r, y1i = wr * y1r - wi * y1i, wr * y1i + wi * y1r
    y2r, y2i = wr * y2r - wi * y2i, wr * y2i + wi * y2r
    for i in range(owned):
        fr, fi = first[i, :half], first[i, half:]
        sr, si = second[i, :half], second[i, half:]
        solution_ref[i, :half] = (y1r * fr - y1i * fi) + (y2r * sr - y2i * si)
        solution_ref[i, half:] = (y1r * fi + y1i * fr) + (y2r * si + y2i * sr)

    factor = 1.0 / (n * owned * width)
    arnoldi_ref[0:1] = as_row(beta * jnp.sqrt(F32(factor)))[:, :half]
    arnoldi_ref[1:2] = as_row(pr)[:, :half]
    arnoldi_ref[2:3] = as_row(pi)[:, :half]
    arnoldi_ref[3:4] = as_row(size_two)[:, :half]

    m1r, m1i, m2r, m2i = (gram[:, k * half : (k + 1) * half] for k in range(4))
    y1r, y1i, y2r, y2i = (as_row(y)[:, :half] for y in (y1r, y1i, y2r, y2i))
    moment_ref[0] = ((y1r * m1r - y1i * m1i) + (y2r * m2r - y2i * m2i)) * factor
    moment_ref[1] = ((y1r * m1i + y1i * m1r) + (y2r * m2i + y2i * m2r)) * factor


def shards(
    n,
    probes,
    near_blocks,
    near_list,
    near_count,
    cluster_rows,
    row_basis,
    col_basis,
    far_list,
    far_coupling,
    weight,
):
    owned, _, nprobe, width = probes.shape
    rows = 2 * nprobe
    slots = near_blocks.shape[1]
    fslots = far_coupling.shape[1]
    rank = far_coupling.shape[3]
    per = width // rank
    groups = fslots // per
    smem = pl.BlockSpec(memory_space=pltpu.SMEM)
    vmem = pl.BlockSpec(memory_space=pltpu.VMEM)
    hbm = pl.BlockSpec(memory_space=pl.ANY)
    field = pltpu.VMEM((owned, rows, width), F32)
    sol, moment, arnoldi = pl.pallas_call(
        functools.partial(kernel, n),
        out_shape=(
            jax.ShapeDtypeStruct((owned, rows, width), F32),
            jax.ShapeDtypeStruct((2, nprobe, nprobe), F32),
            jax.ShapeDtypeStruct((4, nprobe), F32),
        ),
        in_specs=[smem] * 5 + [vmem] * 3 + [hbm] * 2,
        out_specs=(vmem, vmem, vmem),
        scratch_shapes=[
            pltpu.VMEM((owned, slots, 2 * width, width), BF16),
            pltpu.VMEM(far_coupling.shape, F32),
            pltpu.VMEM((owned, groups, 2 * rank, width), BF16),
            pltpu.VMEM((owned, groups, 2 * rank, width), BF16),
            pltpu.VMEM((owned, 2 * width, width), BF16),
            pltpu.VMEM((2, 3 * owned + 1, rows, width), BF16),
            pltpu.VMEM((2, n, owned // per, rows, width), F32),
            pltpu.VMEM((n * owned, rows, width), F32),
            pltpu.VMEM((owned, rows, 2 * width), F32),
            field,
            field,
            field,
            field,
            field,
            pltpu.VMEM((n, 1, width), F32),
            pltpu.VMEM((n, 2, width), F32),
            pltpu.VMEM((n, 1, width), F32),
            pltpu.VMEM((n, nprobe, width), F32),
            pltpu.SemaphoreType.DMA((owned,)),
            pltpu.SemaphoreType.DMA((owned,)),
            pltpu.SemaphoreType.DMA((8, n)),
            pltpu.SemaphoreType.DMA((8, n)),
        ],
        compiler_params=pltpu.CompilerParams(
            collective_id=0, has_side_effects=True, vmem_limit_bytes=60 * 2**20
        ),
    )(
        near_list,
        near_count,
        cluster_rows,
        far_list,
        weight,
        probes.reshape(owned, rows, width),
        row_basis,
        col_basis,
        near_blocks.reshape(owned, slots, 2 * width, width),
        far_coupling,
    )
    return sol.reshape(probes.shape), moment, arnoldi


def solution(mesh):
    in_specs = (
        P("clus", None, None, None),
        P(("contour", "clus"), None, None, None, None),
        P("clus", None),
        P("clus"),
        P("clus"),
        P(("contour", "clus"), None, None, None),
        P(("contour", "clus"), None, None, None),
        P("clus", None),
        P(("contour", "clus"), None, None, None, None),
        P("contour"),
    )
    out_specs = (
        P(("contour", "clus"), None, None, None),
        P("contour", None, None),
        P("contour", None),
    )
    return jax.shard_map(
        functools.partial(shards, mesh.shape["clus"]),
        mesh=mesh,
        in_specs=in_specs,
        out_specs=out_specs,
        check_vma=False,
    )
```
